512 devices in a mesh: row: 16 (over x_lo, y), col: 8 (over z), layer: 4 (over x_hi, core).
Axes of the slice: x: 4 (x_hi: 2, x_lo: 2; x = x_hi * 2 + x_lo), y: 8, z: 8, core: 2. Of those that a mesh axis runs over, the one named last changes fastest.
Arguments:
- edge_values: bfloat16 [8192, 8192], P('row', ('col', 'layer')), as said below
- tile_pattern: int32 [64, 64], P('row', ('col', 'layer')), may hold values from 0 to 1, as said below
Outputs:
- motif: float32 [8192, 8192], P('row', ('col', 'layer'))
The draws below stay inside these ranges and needn't reach their ends.
Inputs may be any that keep to these rules, and one draw needn't show every extreme that they name: `tile_pattern`: 1 marks a stored tile, 0 an empty one; the tiles on the diagonal are always stored; any other tile may be stored, and a tile row or tile column may be stored in full. `edge_values`: edge weights are nonnegative.
All inputs are finite; a program needn't handle non-finite values.
Results may differ from the reference program's by a relative error of at most 0.0003.
Values may be sent and summed in bfloat16 or wider, within the bound.
A program may use at most 64 MiB of HBM per device.

```python
import jax
import jax.numpy as jnp
from jax import lax

TILE = 128
ROWS_DEV = 512
NODES = 8192
COLS_DEV = 256


def draw_tile_pattern(key, part):
    key = jax.random.fold_in(key, 7)
    first_key, second_key, third_key, fourth_key = jax.random.split(key, 4)
    count = NODES // TILE
    row_span = ROWS_DEV // TILE
    col_span = COLS_DEV // TILE
    levels = jax.random.randint(first_key, (count, 1), 4, 24)
    rolls = jax.random.randint(second_key, (count, count), 0, 64)
    row_band = jax.random.randint(third_key, (), 0, NODES // ROWS_DEV)
    col_band = jax.random.randint(fourth_key, (), 0, NODES // COLS_DEV)
    places = jnp.arange(count, dtype=jnp.int32)
    diagonal = places[:, None] == places[None, :]
    full_rows = places // row_span == row_band
    full_cols = places // col_span == col_band
    stored = jnp.logical_or(rolls < levels, diagonal)
    stored = jnp.logical_or(stored, full_rows[:, None])
    stored = jnp.logical_or(stored, full_cols[None, :])
    return stored.astype(jnp.int32)


def draw_edge_values(key, part):
    key = jax.random.fold_in(key, 11)
    height = (64.0 / NODES) ** (1.0 / 3.0)
    unit = jax.random.uniform(key, (NODES, NODES), jnp.float32, 0.0, 1.0)
    values = height * unit
    return values.astype(jnp.bfloat16)


def setup_inputs(seed: int = 0) -> dict:
    arg_keys = jax.random.split(jax.random.key(seed), 3)
    return {
        "edge_values": draw_edge_values(jax.random.fold_in(arg_keys[2], 71), 0),
        "tile_pattern": draw_tile_pattern(jax.random.fold_in(arg_keys[2], 71), 0),
    }


def masked(edge_values, tile_pattern):
    tile_rows, tile_cols = tile_pattern.shape
    height, breadth = edge_values.shape
    tile_size = height // tile_rows
    blocks = edge_values.reshape(tile_rows, tile_size, tile_cols, tile_size)
    keeper = tile_pattern.astype(jnp.bfloat16)[:, None, :, None]
    return (blocks * keeper).reshape(height, breadth)


def reference(edge_values, tile_pattern):
    adjacency = masked(edge_values, tile_pattern)
    dense_adj = adjacency.astype(jnp.float32)
    paths = jnp.dot(dense_adj, dense_adj, precision=lax.Precision.HIGHEST, preferred_element_type=jnp.float32)
    return paths * dense_adj
```

```python
import functools

import jax
import jax.numpy as jnp
from jax import lax
from jax.experimental import pallas as pl
from jax.experimental.pallas import tpu as pltpu
from jax.sharding import PartitionSpec as P

MESH = pl.DeviceIdType.MESH
PARTS = 2
RING = 8


def wrap(d):
    return (d + RING // 2 - 1) % RING - (RING // 2 - 1)


def plan():
    flows = {}

    def add(flow, source, target):
        flows.setdefault(flow, []).append((flow, source, target))

    up = [(0, 0), (0, 1), (0, 2), (0, 3), (1, 0), (1, 2)]
    down = [(0, 0), (0, -1), (0, -2), (1, 0), (1, -1), (1, -2)]
    for side, d in up:
        for s in range(PARTS):
            add("ym", ("C", side, d, s), ("C", side, wrap(d + 1), s))
            add("zm", ("R", side, d, 0, s), ("R", side, wrap(d + 1), 0, s))
    for side, d in down:
        for s in range(PARTS):
            add("yp", ("C", side, d, s), ("C", side, wrap(d - 1), s))
            add("zp", ("R", side, d, 0, s), ("R", side, wrap(d - 1), 0, s))
    for d in (0, 2, 4):
        for s in range(PARTS):
            add("lo", ("C", 0, d, s), ("C", 1, d, s))
            add("hi", ("R", 0, d, 0, s), ("R", 1, d, 0, s))
    return flows


RATE = {"sib": 300e3}


def schedule(flows):
    flows = {name: list(copies) for name, copies in flows.items()}
    size = 512 * 256 * 2 / PARTS
    ready = {}
    for side in (0,):
        for s in range(PARTS):
            ready["C", 0, 0, s] = 0.0
            ready["R", 0, 0, 0, s] = 0.0
    free = {}
    done, order = set(), []
    pending = {name: 0 for name in flows}
    shared = []
    for s in range(PARTS):
        shared.append((0.0, ("R", 0, 0, 0, s)))
    while any(pending[name] < len(flows[name]) for name in flows):
        best = None
        for name in flows:
            if pending[name] < len(flows[name]):
                copy = flows[name][pending[name]]
                if copy[1] in ready:
                    at = ready[copy[1]]
                    if best is None or (at, free.get(name, 0.0)) < best[:2]:
                        best = (at, free.get(name, 0.0), name, copy)
        at, _, name, copy = best
        start = max(at, free.get(name, 0.0))
        end = start + size / RATE.get(name, 50e3) + (1.0 if name != "hi" else 1.5)
        free[name] = end - 1.0
        ready[copy[2]] = end
        order.append((at, copy))
        pending[name] += 1
    for piece, at in ready.items():
        if piece[0] == "R":
            _, h, d, _, s = piece
            order.append((at + 0.01, ("sib", piece, ("R", h, d, 1, s))))
    order.sort(key=lambda entry: entry[0])
    return [copy for _, copy in order]


def kernel(copies, edge_ref, tile_ref, out_ref, rows_ref, cols_ref, total_ref, send_sem, recv_sem):
    row, z, layer = lax.axis_index("row"), lax.axis_index("col"), lax.axis_index("layer")
    x_lo, y = row // RING, row % RING
    x_hi, core = layer // 2, layer % 2
    height, breadth = edge_ref.shape
    part = height // PARTS

    def turn(a, d):
        return (a + (d + RING)) % RING

    devices = {
        "yp": (x_lo * RING + turn(y, 1), z, layer),
        "ym": (x_lo * RING + turn(y, -1), z, layer),
        "zp": (row, turn(z, 1), layer),
        "zm": (row, turn(z, -1), layer),
        "lo": ((1 - x_lo) * RING + y, z, layer),
        "hi": (row, z, (1 - x_hi) * 2 + core),
        "sib": (row, z, x_hi * 2 + 1 - core),
    }
    barrier = pltpu.get_barrier_semaphore()
    for device in devices.values():
        pl.semaphore_signal(barrier, inc=1, device_id=device, device_id_type=MESH)

    tile_rows, tile_cols = tile_ref.shape
    tile = height // tile_rows
    me_r = z * 4 + layer
    for i in range(tile_rows):
        for j in range(tile_cols):
            keeper = tile_ref[i, j].astype(jnp.float32)
            at = (pl.ds(i * tile, tile), pl.ds(j * tile, tile))
            block = (edge_ref[at].astype(jnp.float32) * keeper).astype(jnp.bfloat16)
            rows_ref[(me_r, *at)] = block
            cols_ref[(row, *at)] = block
    pl.semaphore_wait(barrier, len(devices))

    def place(piece):
        span = pl.ds(piece[-1] * part, part)
        if piece[0] == "C":
            _, side, d, _ = piece
            index = (x_lo if side == 0 else 1 - x_lo) * RING + turn(y, d)
            return cols_ref.at[index, span]
        _, h, d, k, _ = piece
        index = turn(z, d) * 4 + (x_hi if h == 0 else 1 - x_hi) * 2 + (core if k == 0 else 1 - core)
        return rows_ref.at[index, span]

    arrivals = {copy[2]: n for n, copy in enumerate(copies)}
    waited = set()

    def arrive(piece):
        if piece not in arrivals or piece in waited:
            return
        waited.add(piece)
        n = arrivals[piece]
        there = place(piece)
        pltpu.make_async_remote_copy(
            src_ref=there, dst_ref=there, send_sem=send_sem.at[n], recv_sem=recv_sem.at[n],
            device_id=devices[copies[n][0]], device_id_type=MESH,
        ).wait_recv()

    started = []
    for n, (flow, source, _) in enumerate(copies):
        arrive(source)
        here = place(source)
        copy = pltpu.make_async_remote_copy(
            src_ref=here, dst_ref=here, send_sem=send_sem.at[n], recv_sem=recv_sem.at[n],
            device_id=devices[flow], device_id_type=MESH,
        )
        copy.start()
        started.append(copy)
    for _, _, target in copies:
        arrive(target)

    half = height // 2
    for m in range(2):
        span = pl.ds(m * half, half)
        total_ref[span, :] = jnp.zeros((half, breadth), jnp.float32)

        def step(j, carry):
            depth = pl.ds((j % 2) * breadth, breadth)
            total_ref[span, :] += jnp.dot(
                rows_ref[j, span, :], cols_ref[j // 2, depth, :], preferred_element_type=jnp.float32
            )
            return carry

        lax.fori_loop(0, rows_ref.shape[0], step, 0)
    out_ref[...] = total_ref[...] * cols_ref[row].astype(jnp.float32)
    for copy in started:
        copy.wait_send()


def shards(edge_values, tile_pattern):
    height, breadth = edge_values.shape
    copies = schedule(plan())
    return pl.pallas_call(
        functools.partial(kernel, copies),
        out_shape=jax.ShapeDtypeStruct((height, breadth), jnp.float32),
        in_specs=[pl.BlockSpec(memory_space=pltpu.VMEM), pl.BlockSpec(memory_space=pltpu.SMEM)],
        out_specs=pl.BlockSpec(memory_space=pltpu.VMEM),
        scratch_shapes=[
            pltpu.VMEM((32, height, breadth), jnp.bfloat16),
            pltpu.VMEM((16, height, breadth), jnp.bfloat16),
            pltpu.VMEM((height, breadth), jnp.float32),
            pltpu.SemaphoreType.DMA((len(copies),)),
            pltpu.SemaphoreType.DMA((len(copies),)),
        ],
        compiler_params=pltpu.CompilerParams(
            collective_id=0, has_side_effects=True, vmem_limit_bytes=24 * 1024 * 1024
        ),
        cost_estimate=pl.CostEstimate(flops=2 * height * 8192 * breadth, bytes_accessed=1 << 20, transcendentals=0),
    )(edge_values, tile_pattern)


def solution(mesh):
    return jax.shard_map(
        shards,
        mesh=mesh,
        in_specs=(P("row", ("col", "layer")), P("row", ("col", "layer"))),
        out_specs=P("row", ("col", "layer")),
        check_vma=False,
    )
```

```python
import jax
import jax.numpy as jnp
from jax import lax
from jax.experimental import pallas as pl
from jax.experimental.pallas import tpu as pltpu
from jax.sharding import PartitionSpec as P

MESH = pl.DeviceIdType.MESH
RING = 8
PARTS = 2
FLOWS = {
    "ym": ("C", 0, 1), "yp": ("C", 0, -1), "lo": ("C", 1, 0),
    "zm": ("R", 0, 1), "zp": ("R", 0, -1), "hi": ("R", 1, 0),
}
STEPS = (
    ("ym", 0, 0, 0), ("yp", 0, 0, 0), ("zm", 0, 0, 0), ("zp", 0, 0, 0), ("lo", 0, 0, 0), ("ym", 0, 0, 1),
    ("yp", 0, 0, 1), ("zm", 0, 0, 1), ("zp", 0, 0, 1), ("lo", 0, 0, 1), ("hi", 0, 0, 0), ("sib", 0, 0, 0),
    ("sib", 0, 0, 1), ("ym", 0, 1, 0), ("yp", 0, -1, 0), ("sib", 0, 1, 0), ("zm", 0, 1, 0), ("sib", 0, -1, 0),
    ("zp", 0, -1, 0), ("ym", 1, 0, 0), ("yp", 1, 0, 0), ("hi", 0, -1, 0), ("ym", 0, 1, 1), ("yp", 0, -1, 1),
    ("sib", 0, 1, 1), ("zm", 0, 1, 1), ("sib", 0, -1, 1), ("zp", 0, -1, 1), ("hi", 0, -1, 1), ("ym", 1, 0, 1),
    ("yp", 1, 0, 1), ("sib", 0, 2, 0), ("lo", 0, -2, 0), ("sib", 0, -2, 0), ("zm", 0, 2, 0), ("zp", 0, -2, 0),
    ("sib", 1, 0, 0), ("zm", 1, 0, 0), ("ym", 0, 2, 0), ("yp", 0, -2, 0), ("sib", 0, 2, 1), ("hi", 0, -2, 0),
    ("sib", 0, -2, 1), ("zm", 0, 2, 1), ("zp", 0, -2, 1), ("mul", 131, 387), ("sib", 1, -1, 0), ("ym", 1, 1, 0),
    ("yp", 0, -2, 1), ("sib", 0, 3, 0), ("zm", 0, 3, 0), ("sib", 0, -3, 0), ("hi", 0, 3, 0), ("sib", 1, -1, 1),
    ("zp", 1, -1, 1), ("ym", 0, 2, 1), ("zm", 1, -1, 1), ("yp", 1, -1, 1), ("sib", 1, 1, 0), ("lo", 0, 2, 1),
    ("sib", 0, -3, 1), ("zp", 0, -3, 1), ("mul", 32967, 33735), ("yp", 1, -2, 0), ("zm", 1, 1, 0),
    ("ym", 0, 3, 0), ("sib", 0, 3, 1), ("lo", 0, 3, 0), ("sib", 1, -2, 1), ("zp", 1, -2, 1), ("sib", 1, -2, 0),
    ("zp", 1, -2, 0), ("yp", 0, -3, 1), ("sib", 0, 4, 0), ("hi", 0, 3, 1), ("sib", 0, 4, 1), ("sib", 1, 3, 0),
    ("zm", 1, 3, 0), ("mul", 49391, 33767), ("yp", 1, -2, 1), ("sib", 1, 0, 1), ("zm", 1, 0, 1), ("sib", 1, -3, 1),
    ("zp", 1, -3, 1), ("ym", 1, 2, 1), ("hi", 0, 2, 1), ("yp", 1, -3, 0), ("sib", 1, 2, 0), ("sib", 1, -3, 0),
    ("mul", 49663, 51183), ("ym", 1, 3, 1), ("sib", 1, 4, 0), ("sib", 1, 4, 1), ("sib", 1, 3, 1),
    ("mul", 57855, 53247), ("sib", 1, 1, 1), ("sib", 1, 2, 1), ("mul", 63999, 61439), ("mul", 65535, 65535),
)


def wrap(d):
    return (d + RING // 2 - 1) % RING - (RING // 2 - 1)


def copies_of(steps):
    copies = []
    for flow, *rest in steps:
        if flow == "sib":
            side, d, s = rest
            copies.append((flow, ("R", side, d, 0, s), ("R", side, d, 1, s)))
        elif flow != "mul":
            side, d, s = rest
            kind, flip, shift = FLOWS[flow]
            core = (0,) if kind == "R" else ()
            copies.append((flow, (kind, side, d, *core, s), (kind, side ^ flip, wrap(d + shift), *core, s)))
    return copies


def kernel(edge_ref, tile_ref, out_ref, rows_ref, cols_ref, total_ref, send_sem, recv_sem):
    row, z, layer = lax.axis_index("row"), lax.axis_index("col"), lax.axis_index("layer")
    x_lo, y = row // RING, row % RING
    x_hi, core = layer // 2, layer % 2
    height, breadth = edge_ref.shape
    part = height // PARTS

    def turn(a, d):
        return (a + (d + RING)) % RING

    devices = {
        "yp": (x_lo * RING + turn(y, 1), z, layer),
        "ym": (x_lo * RING + turn(y, -1), z, layer),
        "zp": (row, turn(z, 1), layer),
        "zm": (row, turn(z, -1), layer),
        "lo": ((1 - x_lo) * RING + y, z, layer),
        "hi": (row, z, (1 - x_hi) * 2 + core),
        "sib": (row, z, x_hi * 2 + 1 - core),
    }
    barrier = pltpu.get_barrier_semaphore()
    for device in devices.values():
        pl.semaphore_signal(barrier, inc=1, device_id=device, device_id_type=MESH)

    tile_rows, tile_cols = tile_ref.shape
    tile = height // tile_rows
    mine = z * 4 + layer
    for i in range(tile_rows):
        for j in range(tile_cols):
            keeper = tile_ref[i, j].astype(jnp.float32)
            at = (pl.ds(i * tile, tile), pl.ds(j * tile, tile))
            block = (edge_ref[at].astype(jnp.float32) * keeper).astype(jnp.bfloat16)
            rows_ref[(mine, *at)] = block
            cols_ref[(row, *at)] = block
    total_ref[...] = jnp.zeros_like(total_ref)
    pl.semaphore_wait(barrier, len(devices))

    def place(piece):
        span = pl.ds(piece[-1] * part, part)
        if piece[0] == "C":
            _, side, d, _ = piece
            index = (x_lo if side == 0 else 1 - x_lo) * RING + turn(y, d)
            return cols_ref.at[index, span]
        _, side, d, k, _ = piece
        index = turn(z, d) * 4 + (x_hi if side == 0 else 1 - x_hi) * 2 + (core if k == 0 else 1 - core)
        return rows_ref.at[index, span]

    copies = copies_of(STEPS)
    arrivals = {copy[2]: n for n, copy in enumerate(copies)}
    waited = set()

    def arrive(piece):
        if piece not in arrivals or piece in waited:
            return
        waited.add(piece)
        n = arrivals[piece]
        there = place(piece)
        pltpu.make_async_remote_copy(
            src_ref=there, dst_ref=there, send_sem=send_sem.at[n], recv_sem=recv_sem.at[n],
            device_id=devices[copies[n][0]], device_id_type=MESH,
        ).wait_recv()

    def multiply(rows, cols, before):
        def step(k, carry):
            r = (k % 2 + x_hi) % 2 * RING + (k // 2 - z + RING) % RING
            c = (k // RING + x_lo) % 2 * RING + (k % RING - y + RING) % RING

            def both(masks):
                return ((masks[0] >> r) % 2) * ((masks[1] >> c) % 2)

            @pl.when(both((rows, cols)) - both(before) == 1)
            def _():
                left = jnp.concatenate([rows_ref[2 * k], rows_ref[2 * k + 1]], axis=1)
                total_ref[...] += jnp.dot(left, cols_ref[k], preferred_element_type=jnp.float32)

            return carry

        lax.fori_loop(0, cols_ref.shape[0], step, 0)

    order = {piece: n for n, piece in enumerate(copy[2] for copy in copies)}
    before, started = (0, 0), []
    for step in STEPS:
        if step[0] == "mul":
            _, rows, cols = step
            ready = [p for p in order if ((rows if p[0] == "R" else cols) >> (RING * p[1] + p[2] % RING)) % 2]
            for piece in ready:
                arrive(piece)
            multiply(rows, cols, before)
            before = (rows, cols)
            continue
        n = len(started)
        flow, source, _ = copies[n]
        arrive(source)
        here = place(source)
        copy = pltpu.make_async_remote_copy(
            src_ref=here, dst_ref=here, send_sem=send_sem.at[n], recv_sem=recv_sem.at[n],
            device_id=devices[flow], device_id_type=MESH,
        )
        copy.start()
        started.append(copy)
    out_ref[...] = total_ref[...] * cols_ref[row].astype(jnp.float32)
    for copy in started:
        copy.wait_send()


def shards(edge_values, tile_pattern):
    height, breadth = edge_values.shape
    count = len(copies_of(STEPS))
    return pl.pallas_call(
        kernel,
        out_shape=jax.ShapeDtypeStruct((height, breadth), jnp.float32),
        in_specs=[pl.BlockSpec(memory_space=pltpu.VMEM), pl.BlockSpec(memory_space=pltpu.SMEM)],
        out_specs=pl.BlockSpec(memory_space=pltpu.VMEM),
        scratch_shapes=[
            pltpu.VMEM((32, height, breadth), jnp.bfloat16),
            pltpu.VMEM((16, height, breadth), jnp.bfloat16),
            pltpu.VMEM((height, breadth), jnp.float32),
            pltpu.SemaphoreType.DMA((count,)),
            pltpu.SemaphoreType.DMA((count,)),
        ],
        compiler_params=pltpu.CompilerParams(
            collective_id=0, has_side_effects=True, vmem_limit_bytes=24 * 1024 * 1024
        ),
        cost_estimate=pl.CostEstimate(flops=2 * height * 8192 * breadth, bytes_accessed=1 << 20, transcendentals=0),
    )(edge_values, tile_pattern)


def solution(mesh):
    return jax.shard_map(
        shards,
        mesh=mesh,
        in_specs=(P("row", ("col", "layer")), P("row", ("col", "layer"))),
        out_specs=P("row", ("col", "layer")),
        check_vma=False,
    )
```

```python
import jax
import jax.numpy as jnp
from jax import lax
from jax.experimental import pallas as pl
from jax.experimental.pallas import tpu as pltpu
from jax.sharding import PartitionSpec as P

MESH = pl.DeviceIdType.MESH
RING = 8
CUTS = (0, 128, 256, 384, 512)
LAG = 64
FLOWS = {
    "ym": ("C", 0, 1), "yp": ("C", 0, -1), "lo": ("C", 1, 0),
    "zm": ("R", 0, 1), "zp": ("R", 0, -1), "hi": ("R", 1, 0),
}
STEPS = (
    ("ym", 0, 0, 0), ("yp", 0, 0, 0), ("zm", 0, 0, 0), ("zp", 0, 0, 0), ("lo", 0, 0, 0), ("ym", 0, 0, 1),
    ("yp", 0, 0, 1), ("zm", 0, 0, 1), ("zp", 0, 0, 1), ("lo", 0, 0, 1), ("ym", 0, 0, 2), ("yp", 0, 0, 2),
    ("zm", 0, 0, 2), ("zp", 0, 0, 2), ("lo", 0, 0, 2), ("ym", 0, 0, 3), ("yp", 0, 0, 3), ("zm", 0, 0, 3),
    ("zp", 0, 0, 3), ("lo", 0, 0, 3), ("sib", 0, 0, 0, 4), ("hi", 0, 0, 0), ("ym", 0, 1, 0), ("yp", 0, -1, 0),
    ("zm", 0, 1, 0), ("zp", 0, -1, 0), ("ym", 1, 0, 0), ("yp", 1, 0, 0), ("hi", 0, -1, 0), ("zm", 0, 1, 1),
    ("zp", 0, -1, 1), ("ym", 1, 0, 1), ("yp", 1, 0, 1), ("hi", 0, -1, 1), ("zm", 0, 1, 2), ("zp", 0, -1, 2),
    ("ym", 1, 0, 2), ("yp", 1, 0, 2), ("hi", 0, -1, 2), ("sib", 0, 1, 0, 4), ("zm", 0, 1, 3), ("sib", 0, -1, 0, 4),
    ("zp", 0, -1, 3), ("ym", 1, 0, 3), ("yp", 1, 0, 3), ("hi", 0, -1, 3), ("zm", 0, 2, 0), ("zp", 0, -2, 0),
    ("ym", 0, 2, 0), ("yp", 0, -2, 0), ("lo", 0, -2, 0), ("zm", 1, 0, 0), ("zp", 0, -2, 1), ("ym", 0, 1, 1),
    ("yp", 0, -1, 1), ("zm", 0, 2, 1), ("hi", 0, 2, 0), ("zp", 1, -1, 0), ("mul", 131, 387), ("ym", 0, 1, 2),
    ("yp", 1, -1, 1), ("zm", 0, 2, 2), ("zp", 0, -2, 2), ("hi", 0, 2, 1), ("sib", 0, 2, 0, 4), ("sib", 0, -2, 0, 4),
    ("ym", 0, 1, 3), ("yp", 1, -1, 2), ("zm", 1, -1, 1), ("zp", 1, -1, 1), ("hi", 0, 2, 2), ("sib", 0, -3, 0, 1),
    ("ym", 1, 1, 0), ("yp", 0, -1, 2), ("zm", 1, -1, 2), ("mul", 131, 33667), ("zp", 1, -1, 2), ("hi", 0, 2, 3),
    ("sib", 1, -1, 0, 4), ("sib", 0, -3, 1, 1), ("ym", 0, 3, 0), ("yp", 1, -1, 3), ("zm", 1, -1, 3),
    ("zp", 1, -1, 3), ("hi", 0, -3, 0), ("ym", 0, 2, 1), ("yp", 0, -2, 1), ("zm", 0, 2, 3), ("zp", 0, -3, 0),
    ("lo", 0, -3, 0), ("sib", 0, -3, 2, 1), ("ym", 0, 2, 2), ("mul", 32967, 33667), ("yp", 0, -1, 3),
    ("zm", 1, 2, 0), ("zp", 0, -3, 1), ("hi", 0, -3, 1), ("ym", 0, 2, 3), ("yp", 1, -2, 1), ("zm", 1, 2, 1),
    ("zp", 1, 2, 1), ("hi", 0, -3, 2), ("ym", 1, 1, 1), ("yp", 0, -2, 2), ("zm", 1, 2, 2), ("mul", 32967, 33671),
    ("zp", 1, 2, 2), ("lo", 0, 2, 2), ("sib", 1, 2, 0, 4), ("sib", 1, 0, 0, 4), ("sib", 1, -2, 0, 4),
    ("ym", 1, 1, 3), ("yp", 1, -2, 2), ("zm", 1, 2, 3), ("zp", 1, -2, 3), ("lo", 0, 4, 0), ("sib", 0, 3, 0, 4),
    ("sib", 0, 4, 0, 1), ("ym", 0, 3, 1), ("yp", 1, -2, 3), ("zm", 1, 0, 3), ("zp", 0, -3, 2), ("hi", 0, 4, 0),
    ("mul", 32967, 50055), ("sib", 0, 4, 1, 1), ("ym", 0, 3, 2), ("yp", 0, -2, 3), ("zm", 0, 3, 3),
    ("zp", 0, -2, 3), ("hi", 0, 4, 1), ("ym", 0, 3, 3), ("yp", 1, -3, 1), ("lo", 0, 3, 0), ("zp", 1, -3, 2),
    ("mul", 50639, 50127), ("ym", 1, 2, 1), ("lo", 0, 3, 2), ("yp", 1, -3, 2), ("sib", 1, 3, 0, 4),
    ("zm", 1, 3, 3), ("sib", 1, -3, 0, 4), ("mul", 50639, 50127), ("ym", 1, 2, 3), ("yp", 1, -3, 3),
    ("sib", 1, 1, 0, 4), ("sib", 0, 4, 2, 1), ("mul", 50639, 59343), ("sib", 1, 4, 0, 1), ("sib", 0, 4, 3, 1),
    ("sib", 0, -3, 3, 1), ("sib", 1, 4, 1, 1), ("sib", 1, 4, 3, 1), ("sib", 1, 4, 2, 1), ("mul", 61391, 59375),
    ("mul", 61439, 59391), ("mul", 65535, 65535),
)


def wrap(d):
    return (d + RING // 2 - 1) % RING - (RING // 2 - 1)


def copies_of(steps):
    copies = []
    for flow, *rest in steps:
        if flow == "sib":
            side, d, s, n = rest
            copies.append((flow, ("R", side, d, 0, (s, n)), ("R", side, d, 1, (s, n))))
        elif flow != "mul":
            side, d, s = rest
            kind, flip, shift = FLOWS[flow]
            core = (0,) if kind == "R" else ()
            copies.append((flow, (kind, side, d, *core, s), (kind, side ^ flip, wrap(d + shift), *core, s)))
    return copies


def kernel(edge_hbm, tile_hbm, out_ref, edge_ref, tile_ref, turn_ref, rows_ref, cols_ref, total_ref, load_sem, send_sem, recv_sem):
    row, z, layer = lax.axis_index("row"), lax.axis_index("col"), lax.axis_index("layer")
    x_lo, y = row // RING, row % RING
    x_hi, core = layer // 2, layer % 2
    height, breadth = edge_ref.shape

    def turn(a, d):
        return (a + (d + RING)) % RING

    devices = {
        "yp": (x_lo * RING + turn(y, 1), z, layer),
        "ym": (x_lo * RING + turn(y, -1), z, layer),
        "zp": (row, turn(z, 1), layer),
        "zm": (row, turn(z, -1), layer),
        "lo": ((1 - x_lo) * RING + y, z, layer),
        "hi": (row, z, (1 - x_hi) * 2 + core),
        "sib": (row, z, x_hi * 2 + 1 - core),
    }
    barrier = pltpu.get_barrier_semaphore()
    for device in devices.values():
        pl.semaphore_signal(barrier, inc=1, device_id=device, device_id_type=MESH)

    loads = [
        pltpu.make_async_copy(tile_hbm, tile_ref, load_sem.at[0]),
        pltpu.make_async_copy(edge_hbm, edge_ref, load_sem.at[1]),
    ]
    for load in loads:
        load.start()
    for load in loads:
        load.wait()
    tile_cols, tile_rows = tile_ref.shape
    tile = height // tile_rows
    mine = z * 4 + layer
    for i in range(tile_rows):
        for j in range(tile_cols):
            stored = tile_ref[j, i] == 1
            at = (pl.ds(i * tile, tile), pl.ds(j * tile, tile))
            block = edge_ref[at]
            block = jnp.where(stored, block, jnp.zeros_like(block))
            rows_ref[(mine, *at)] = block
            cols_ref[(row, *at)] = block
    pl.semaphore_wait(barrier, len(devices))

    def place(piece):
        first, parts = piece[-1] if isinstance(piece[-1], tuple) else (piece[-1], 1)
        span = pl.ds(CUTS[first], CUTS[first + parts] - CUTS[first])
        if piece[0] == "C":
            _, side, d, _ = piece
            index = (x_lo if side == 0 else 1 - x_lo) * RING + turn(y, d)
            return cols_ref.at[index, span]
        _, side, d, k, _ = piece
        index = turn(z, d) * 4 + (x_hi if side == 0 else 1 - x_hi) * 2 + (core if k == 0 else 1 - core)
        return rows_ref.at[index, span]

    copies = copies_of(STEPS)
    arrivals = {copy[2]: n for n, copy in enumerate(copies)}
    waited = set()

    def arrive(piece):
        if piece not in arrivals or piece in waited:
            return
        waited.add(piece)
        n = arrivals[piece]
        there = place(piece)
        pltpu.make_async_remote_copy(
            src_ref=there, dst_ref=there, send_sem=send_sem.at[n], recv_sem=recv_sem.at[n],
            device_id=devices[copies[n][0]], device_id_type=MESH,
        ).wait_recv()

    def rank(k, carry):
        r = (k % 2 + x_hi) % 2 * RING + (k // 2 - z + RING) % RING
        c = (k // RING + x_lo) % 2 * RING + (k % RING - y + RING) % RING
        late = 0
        for rows, cols in turns[:-1]:
            late = late + 1 - ((rows >> r) % 2) * ((cols >> c) % 2)
        turn_ref[k] = late
        return carry

    def multiply(now):
        def step(k, carry):
            @pl.when(turn_ref[k] == now)
            def _():
                left = jnp.concatenate([rows_ref[2 * k], rows_ref[2 * k + 1]], axis=1)
                total_ref[...] += jnp.dot(left, cols_ref[k], preferred_element_type=jnp.float32)

            return carry

        lax.fori_loop(0, cols_ref.shape[0], step, 0)

    order = {piece: n for n, piece in enumerate(copy[2] for copy in copies)}
    turns, started, now = [step[1:] for step in STEPS if step[0] == "mul"], [], 0
    for step in STEPS:
        if step[0] == "mul":
            _, rows, cols = step
            ready = [p for p in order if ((rows if p[0] == "R" else cols) >> (RING * p[1] + p[2] % RING)) % 2]
            for piece in ready:
                arrive(piece)
            if now == 0:
                total_ref[...] = jnp.zeros_like(total_ref)
                lax.fori_loop(0, cols_ref.shape[0], rank, 0)
            multiply(now)
            now += 1
            continue
        n = len(started)
        flow, source, _ = copies[n]
        if flow == "sib":
            for s in range(source[-1][0], sum(source[-1])):
                arrive((*source[:-1], s))
        else:
            arrive(source)
        here = place(source)
        copy = pltpu.make_async_remote_copy(
            src_ref=here, dst_ref=here, send_sem=send_sem.at[n], recv_sem=recv_sem.at[n],
            device_id=devices[flow], device_id_type=MESH,
        )
        copy.start()
        started.append(copy)
        if n >= LAG:
            started[n - LAG].wait_send()
    out_ref[...] = total_ref[...] * cols_ref[row].astype(jnp.float32)
    for copy in started[-LAG:]:
        copy.wait_send()


def shards(edge_values, tile_pattern):
    height, breadth = edge_values.shape
    count = len(copies_of(STEPS))
    return pl.pallas_call(
        kernel,
        out_shape=jax.ShapeDtypeStruct((height, breadth), jnp.float32),
        in_specs=[pl.BlockSpec(memory_space=pl.ANY), pl.BlockSpec(memory_space=pl.ANY)],
        out_specs=pl.BlockSpec(memory_space=pltpu.VMEM),
        scratch_shapes=[
            pltpu.VMEM((height, breadth), edge_values.dtype),
            pltpu.SMEM(tile_pattern.shape[::-1], tile_pattern.dtype),
            pltpu.SMEM((16,), jnp.int32),
            pltpu.VMEM((32, height, breadth), jnp.bfloat16),
            pltpu.VMEM((16, height, breadth), jnp.bfloat16),
            pltpu.VMEM((height, breadth), jnp.float32),
            pltpu.SemaphoreType.DMA((2,)),
            pltpu.SemaphoreType.DMA((count,)),
            pltpu.SemaphoreType.DMA((count,)),
        ],
        compiler_params=pltpu.CompilerParams(
            collective_id=0, has_side_effects=True, vmem_limit_bytes=60 * 1024 * 1024
        ),
        cost_estimate=pl.CostEstimate(flops=2 * height * 8192 * breadth, bytes_accessed=1 << 20, transcendentals=0),
    )(edge_values, tile_pattern.T)


def solution(mesh):
    return jax.shard_map(
        shards,
        mesh=mesh,
        in_specs=(P("row", ("col", "layer")), P("row", ("col", "layer"))),
        out_specs=P("row", ("col", "layer")),
        check_vma=False,
    )
```

```python
import jax
import jax.numpy as jnp
from jax import lax
from jax.experimental import pallas as pl
from jax.experimental.pallas import tpu as pltpu
from jax.sharding import PartitionSpec as P

MESH = pl.DeviceIdType.MESH
RING = 8
CUTS = (0, 128, 256, 384, 512)
LAG = 64
FLOWS = {
    "ym": ("C", 0, 1), "yp": ("C", 0, -1), "lo": ("C", 1, 0),
    "zm": ("R", 0, 1), "zp": ("R", 0, -1), "hi": ("R", 1, 0),
}
STEPS = (
    ("ym", 0, 0, 0), ("yp", 0, 0, 0), ("zm", 0, 0, 0), ("zp", 0, 0, 0), ("lo", 0, 0, 0), ("ym", 0, 0, 1),
    ("yp", 0, 0, 1), ("zm", 0, 0, 1), ("zp", 0, 0, 1), ("lo", 0, 0, 1), ("ym", 0, 0, 2), ("yp", 0, 0, 2),
    ("zm", 0, 0, 2), ("zp", 0, 0, 2), ("lo", 0, 0, 2), ("ym", 0, 0, 3), ("yp", 0, 0, 3), ("zm", 0, 0, 3),
    ("zp", 0, 0, 3), ("lo", 0, 0, 3), ("sib", 0, 0, 0, 4), ("hi", 0, 0, 0), ("ym", 0, 1, 0), ("yp", 0, -1, 0),
    ("zm", 0, 1, 0), ("zp", 0, -1, 0), ("ym", 1, 0, 0), ("yp", 1, 0, 0), ("hi", 0, -1, 0), ("zm", 0, 1, 1),
    ("zp", 0, -1, 1), ("ym", 1, 0, 1), ("yp", 1, 0, 1), ("hi", 0, -1, 1), ("zm", 0, 1, 2), ("zp", 0, -1, 2),
    ("ym", 1, 0, 2), ("yp", 1, 0, 2), ("hi", 0, -1, 2), ("sib", 0, 1, 0, 4), ("zm", 0, 1, 3), ("sib", 0, -1, 0, 4),
    ("zp", 0, -1, 3), ("ym", 1, 0, 3), ("yp", 1, 0, 3), ("hi", 0, -1, 3), ("zm", 0, 2, 0), ("zp", 0, -2, 0),
    ("ym", 0, 2, 0), ("yp", 0, -2, 0), ("lo", 0, -2, 0), ("zm", 1, 0, 0), ("zp", 0, -2, 1), ("ym", 0, 1, 1),
    ("yp", 0, -1, 1), ("zm", 0, 2, 1), ("hi", 0, 2, 0), ("zp", 1, -1, 0), ("mul", 131, 387), ("ym", 0, 1, 2),
    ("yp", 1, -1, 1), ("zm", 0, 2, 2), ("zp", 0, -2, 2), ("hi", 0, 2, 1), ("sib", 0, 2, 0, 4), ("sib", 0, -2, 0, 4),
    ("ym", 0, 1, 3), ("yp", 1, -1, 2), ("zm", 1, -1, 1), ("zp", 1, -1, 1), ("hi", 0, 2, 2), ("sib", 0, -3, 0, 1),
    ("ym", 1, 1, 0), ("yp", 0, -1, 2), ("zm", 1, -1, 2), ("mul", 131, 33667), ("zp", 1, -1, 2), ("hi", 0, 2, 3),
    ("sib", 1, -1, 0, 4), ("sib", 0, -3, 1, 1), ("ym", 0, 3, 0), ("yp", 1, -1, 3), ("zm", 1, -1, 3),
    ("zp", 1, -1, 3), ("hi", 0, -3, 0), ("ym", 0, 2, 1), ("yp", 0, -2, 1), ("zm", 0, 2, 3), ("zp", 0, -3, 0),
    ("lo", 0, -3, 0), ("sib", 0, -3, 2, 1), ("ym", 0, 2, 2), ("mul", 32967, 33667), ("yp", 0, -1, 3),
    ("zm", 1, 2, 0), ("zp", 0, -3, 1), ("hi", 0, -3, 1), ("ym", 0, 2, 3), ("yp", 1, -2, 1), ("zm", 1, 2, 1),
    ("zp", 1, 2, 1), ("hi", 0, -3, 2), ("ym", 1, 1, 1), ("yp", 0, -2, 2), ("zm", 1, 2, 2), ("mul", 32967, 33671),
    ("zp", 1, 2, 2), ("lo", 0, 2, 2), ("sib", 1, 2, 0, 4), ("sib", 1, 0, 0, 4), ("sib", 1, -2, 0, 4),
    ("ym", 1, 1, 3), ("yp", 1, -2, 2), ("zm", 1, 2, 3), ("zp", 1, -2, 3), ("lo", 0, 4, 0), ("sib", 0, 3, 0, 4),
    ("sib", 0, 4, 0, 1), ("ym", 0, 3, 1), ("yp", 1, -2, 3), ("zm", 1, 0, 3), ("zp", 0, -3, 2), ("hi", 0, 4, 0),
    ("mul", 32967, 50055), ("sib", 0, 4, 1, 1), ("ym", 0, 3, 2), ("yp", 0, -2, 3), ("zm", 0, 3, 3),
    ("zp", 0, -2, 3), ("hi", 0, 4, 1), ("ym", 0, 3, 3), ("yp", 1, -3, 1), ("lo", 0, 3, 0), ("zp", 1, -3, 2),
    ("mul", 50639, 50127), ("ym", 1, 2, 1), ("lo", 0, 3, 2), ("yp", 1, -3, 2), ("sib", 1, 3, 0, 4),
    ("zm", 1, 3, 3), ("sib", 1, -3, 0, 4), ("mul", 50639, 50127), ("ym", 1, 2, 3), ("yp", 1, -3, 3),
    ("sib", 1, 1, 0, 4), ("sib", 0, 4, 2, 1), ("mul", 50639, 59343), ("sib", 1, 4, 0, 1), ("sib", 0, 4, 3, 1),
    ("sib", 0, -3, 3, 1), ("sib", 1, 4, 1, 1), ("sib", 1, 4, 3, 1), ("sib", 1, 4, 2, 1), ("mul", 61391, 59375),
    ("mul", 61439, 59391), ("mul", 65535, 65535),
)


def wrap(d):
    return (d + RING // 2 - 1) % RING - (RING // 2 - 1)


def copies_of(steps):
    copies = []
    for flow, *rest in steps:
        if flow == "sib":
            side, d, s, n = rest
            copies.append((flow, ("R", side, d, 0, (s, n)), ("R", side, d, 1, (s, n))))
        elif flow != "mul":
            side, d, s = rest
            kind, flip, shift = FLOWS[flow]
            core = (0,) if kind == "R" else ()
            copies.append((flow, (kind, side, d, *core, s), (kind, side ^ flip, wrap(d + shift), *core, s)))
    return copies


def kernel(edge_hbm, tile_hbm, out_ref, edge_ref, tile_ref, turn_ref, rows_ref, cols_ref, total_ref, load_sem, send_sem, recv_sem):
    row, z, layer = lax.axis_index("row"), lax.axis_index("col"), lax.axis_index("layer")
    x_lo, y = row // RING, row % RING
    x_hi, core = layer // 2, layer % 2
    height, breadth = edge_ref.shape

    def turn(a, d):
        return (a + (d + RING)) % RING

    devices = {
        "yp": (x_lo * RING + turn(y, 1), z, layer),
        "ym": (x_lo * RING + turn(y, -1), z, layer),
        "zp": (row, turn(z, 1), layer),
        "zm": (row, turn(z, -1), layer),
        "lo": ((1 - x_lo) * RING + y, z, layer),
        "hi": (row, z, (1 - x_hi) * 2 + core),
        "sib": (row, z, x_hi * 2 + 1 - core),
    }
    barrier = pltpu.get_barrier_semaphore()
    for device in devices.values():
        pl.semaphore_signal(barrier, inc=1, device_id=device, device_id_type=MESH)

    loads = [
        pltpu.make_async_copy(tile_hbm, tile_ref, load_sem.at[0]),
        pltpu.make_async_copy(edge_hbm, edge_ref, load_sem.at[1]),
    ]
    for load in loads:
        load.start()
    for load in loads:
        load.wait()
    tile_cols, tile_rows = tile_ref.shape
    tile = height // tile_rows
    mine = z * 4 + layer
    for i in range(tile_rows):
        for j in range(tile_cols):
            stored = tile_ref[j, i] == 1
            at = (pl.ds(i * tile, tile), pl.ds(j * tile, tile))
            block = edge_ref[at]
            block = jnp.where(stored, block, jnp.zeros_like(block))
            rows_ref[(mine, *at)] = block
            cols_ref[(row, *at)] = block
    pl.semaphore_wait(barrier, len(devices))

    def place(piece):
        first, parts = piece[-1] if isinstance(piece[-1], tuple) else (piece[-1], 1)
        span = pl.ds(CUTS[first], CUTS[first + parts] - CUTS[first])
        if piece[0] == "C":
            _, side, d, _ = piece
            index = (x_lo if side == 0 else 1 - x_lo) * RING + turn(y, d)
            return cols_ref.at[index, span]
        _, side, d, k, _ = piece
        index = turn(z, d) * 4 + (x_hi if side == 0 else 1 - x_hi) * 2 + (core if k == 0 else 1 - core)
        return rows_ref.at[index, span]

    copies = copies_of(STEPS)
    arrivals = {copy[2]: n for n, copy in enumerate(copies)}
    waited = set()

    def arrive(piece):
        if piece not in arrivals or piece in waited:
            return
        waited.add(piece)
        n = arrivals[piece]
        there = place(piece)
        pltpu.make_async_remote_copy(
            src_ref=there, dst_ref=there, send_sem=send_sem.at[n], recv_sem=recv_sem.at[n],
            device_id=devices[copies[n][0]], device_id_type=MESH,
        ).wait_recv()

    def rank(k, carry):
        r = (k % 2 + x_hi) % 2 * RING + (k // 2 - z + RING) % RING
        c = (k // RING + x_lo) % 2 * RING + (k % RING - y + RING) % RING
        late = 0
        for rows, cols in turns[:-1]:
            late = late + 1 - ((rows >> r) % 2) * ((cols >> c) % 2)
        turn_ref[k] = late
        return carry

    def multiply(now):
        def step(k, carry):
            @pl.when(turn_ref[k] == now)
            def _():
                left = jnp.concatenate([rows_ref[2 * k], rows_ref[2 * k + 1]], axis=1)
                total_ref[...] += jnp.dot(left, cols_ref[k], preferred_element_type=jnp.float32)

            return carry

        lax.fori_loop(0, cols_ref.shape[0], step, 0)

    order = {piece: n for n, piece in enumerate(copy[2] for copy in copies)}
    turns, started, now = [step[1:] for step in STEPS if step[0] == "mul"], [], 0
    for step in STEPS:
        if step[0] == "mul":
            _, rows, cols = step
            ready = [p for p in order if ((rows if p[0] == "R" else cols) >> (RING * p[1] + p[2] % RING)) % 2]
            for piece in ready:
                arrive(piece)
            if now == 0:
                total_ref[...] = jnp.zeros_like(total_ref)
                lax.fori_loop(0, cols_ref.shape[0], rank, 0)
            multiply(now)
            now += 1
            continue
        n = len(started)
        flow, source, _ = copies[n]
        if flow == "sib":
            for s in range(source[-1][0], sum(source[-1])):
                arrive((*source[:-1], s))
        else:
            arrive(source)
        here = place(source)
        copy = pltpu.make_async_remote_copy(
            src_ref=here, dst_ref=here, send_sem=send_sem.at[n], recv_sem=recv_sem.at[n],
            device_id=devices[flow], device_id_type=MESH,
        )
        copy.start()
        started.append(copy)
        if n >= LAG:
            started[n - LAG].wait_send()
    out_ref[...] = total_ref[...] * cols_ref[row].astype(jnp.float32)
    for copy in started[-LAG:]:
        copy.wait_send()


def shards(edge_values, tile_pattern):
    height, breadth = edge_values.shape
    count = len(copies_of(STEPS))
    return pl.pallas_call(
        kernel,
        out_shape=jax.ShapeDtypeStruct((height, breadth), jnp.float32),
        in_specs=[pl.BlockSpec(memory_space=pl.ANY), pl.BlockSpec(memory_space=pl.ANY)],
        out_specs=pl.BlockSpec(memory_space=pltpu.VMEM),
        scratch_shapes=[
            pltpu.VMEM((height, breadth), edge_values.dtype),
            pltpu.SMEM(tile_pattern.shape[::-1], tile_pattern.dtype),
            pltpu.SMEM((16,), jnp.int32),
            pltpu.VMEM((32, height, breadth), jnp.bfloat16),
            pltpu.VMEM((16, height, breadth), jnp.bfloat16),
            pltpu.VMEM((height, breadth), jnp.float32),
            pltpu.SemaphoreType.DMA((2,)),
            pltpu.SemaphoreType.DMA((count,)),
            pltpu.SemaphoreType.DMA((count,)),
        ],
        compiler_params=pltpu.CompilerParams(
            collective_id=0, has_side_effects=True, vmem_limit_bytes=24 * 1024 * 1024
        ),
        cost_estimate=pl.CostEstimate(flops=2 * height * 8192 * breadth, bytes_accessed=1 << 20, transcendentals=0),
    )(*(pltpu.with_memory_space_constraint(x, pltpu.HBM) for x in (edge_values, tile_pattern.T)))


def solution(mesh):
    return jax.shard_map(
        shards,
        mesh=mesh,
        in_specs=(P("row", ("col", "layer")), P("row", ("col", "layer"))),
        out_specs=P("row", ("col", "layer")),
        check_vma=False,
    )
```

```python
import jax
import jax.numpy as jnp
from jax import lax
from jax.experimental import pallas as pl
from jax.experimental.pallas import tpu as pltpu
from jax.sharding import PartitionSpec as P

MESH = pl.DeviceIdType.MESH
RING = 8
BLOCKS = 16
CUTS = (0, 128, 256, 384, 512)
LAG, LAST = 28, 8
FLOWS = {
    "ym": ("C", 0, 1), "yp": ("C", 0, -1), "lo": ("C", 1, 0),
    "zm": ("R", 0, 1), "zp": ("R", 0, -1), "hi": ("R", 1, 0),
}
STEPS = (
    ("ym", 0, 0, 0), ("yp", 0, 0, 0), ("zm", 0, 0, 0), ("zp", 0, 0, 0), ("lo", 0, 0, 0), ("ym", 0, 0, 1),
    ("yp", 0, 0, 1), ("zm", 0, 0, 1), ("zp", 0, 0, 1), ("lo", 0, 0, 1), ("ym", 0, 0, 2), ("yp", 0, 0, 2),
    ("zm", 0, 0, 2), ("zp", 0, 0, 2), ("lo", 0, 0, 2), ("ym", 0, 0, 3), ("yp", 0, 0, 3), ("zm", 0, 0, 3),
    ("zp", 0, 0, 3), ("lo", 0, 0, 3), ("sib", 0, 0, 0, 4), ("hi", 0, 0, 0), ("ym", 0, 1, 0), ("yp", 0, -1, 0),
    ("zm", 0, 1, 0), ("zp", 0, -1, 0), ("ym", 1, 0, 0), ("yp", 1, 0, 0), ("hi", 0, 1, 0), ("zm", 0, 1, 1),
    ("ym", 0, 1, 1), ("zp", 0, -1, 1), ("yp", 0, -1, 1), ("hi", 0, 1, 1), ("zm", 0, 1, 2), ("zp", 0, -1, 2),
    ("ym", 1, 0, 1), ("yp", 0, -1, 2), ("lo", 0, -1, 1), ("sib", 0, 1, 0, 4), ("zm", 0, 1, 3), ("sib", 0, -1, 0, 4),
    ("zp", 0, -1, 3), ("ym", 1, 0, 2), ("yp", 0, -1, 3), ("hi", 0, 1, 2), ("zm", 0, 2, 0), ("zp", 0, -2, 0),
    ("ym", 1, 0, 3), ("yp", 1, 0, 2), ("hi", 0, 1, 3), ("zp", 1, 0, 0), ("zm", 0, 2, 1), ("ym", 1, 1, 0),
    ("yp", 1, 0, 3), ("zp", 0, -2, 1), ("hi", 0, -2, 0), ("zm", 1, 1, 0), ("mul", 131, 387), ("ym", 0, 1, 2),
    ("yp", 0, -2, 0), ("zm", 0, 2, 2), ("zp", 0, -2, 2), ("hi", 0, -2, 1), ("sib", 0, 2, 0, 4), ("ym", 1, 1, 1),
    ("sib", 0, -2, 0, 4), ("yp", 0, -2, 1), ("zm", 0, 2, 3), ("zp", 1, 1, 1), ("hi", 0, -2, 2), ("ym", 1, 1, 2),
    ("yp", 0, -2, 2), ("zm", 1, 1, 1), ("zp", 0, -3, 0), ("hi", 0, 3, 0), ("mul", 131, 451), ("ym", 1, 1, 3),
    ("yp", 0, -2, 3), ("zm", 1, 1, 2), ("zp", 1, 1, 2), ("hi", 0, 3, 1), ("sib", 1, 1, 0, 4), ("ym", 0, 1, 3),
    ("yp", 1, -1, 0), ("zm", 1, 1, 3), ("zp", 1, 1, 3), ("hi", 0, -2, 3), ("ym", 1, 2, 0), ("yp", 0, -3, 0),
    ("zm", 0, 3, 1), ("zp", 1, -2, 0), ("hi", 0, 3, 2), ("mul", 199, 33731), ("sib", 0, 3, 0, 4),
    ("ym", 1, 2, 1), ("yp", 0, -3, 1), ("zm", 1, -2, 1), ("zp", 1, -2, 1), ("hi", 0, 3, 3), ("ym", 1, 2, 2),
    ("yp", 0, -3, 2), ("zm", 1, -2, 2), ("zp", 1, -2, 2), ("lo", 0, -3, 0), ("mul", 711, 33731), ("ym", 1, 2, 3),
    ("yp", 0, -3, 3), ("zm", 0, 3, 2), ("zp", 0, -2, 3), ("lo", 0, -3, 1), ("sib", 1, 2, 0, 4), ("ym", 0, 2, 0),
    ("sib", 1, 0, 0, 4), ("yp", 1, -1, 1), ("zm", 0, 3, 3), ("zp", 1, 0, 3), ("lo", 0, -3, 2), ("mul", 719, 34791),
    ("sib", 1, -2, 0, 4), ("ym", 1, 3, 0), ("sib", 1, -3, 0, 1), ("yp", 1, -1, 2), ("zm", 1, 3, 0),
    ("zp", 1, -2, 3), ("lo", 0, -3, 3), ("ym", 1, 3, 1), ("sib", 1, -3, 1, 1), ("yp", 0, 4, 1), ("zm", 1, 3, 1),
    ("lo", 0, -2, 3), ("sib", 1, 3, 0, 4), ("mul", 18383, 34791), ("ym", 1, 3, 2), ("sib", 1, -3, 2, 1),
    ("zp", 1, -3, 2), ("yp", 0, 4, 2), ("zm", 1, 3, 3), ("lo", 0, 4, 3), ("ym", 0, 2, 3), ("sib", 0, -3, 0, 4),
    ("mul", 18383, 34791), ("sib", 0, 4, 0, 4), ("sib", 1, -1, 0, 4), ("mul", 20431, 36855), ("sib", 1, 4, 0, 1),
    ("sib", 1, -3, 3, 1), ("sib", 1, 4, 1, 1), ("sib", 1, 4, 2, 1), ("mul", 20479, 45047), ("sib", 1, 4, 3, 1),
    ("mul", 61439, 61431), ("mul", 65535, 65535),
)


def wrap(d):
    return (d + RING // 2 - 1) % RING - (RING // 2 - 1)


def copies_of(steps):
    copies = []
    for flow, *rest in steps:
        if flow == "sib":
            side, d, s, n = rest
            copies.append((flow, ("R", side, d, 0, (s, n)), ("R", side, d, 1, (s, n))))
        elif flow != "mul":
            side, d, s = rest
            kind, flip, shift = FLOWS[flow]
            core = (0,) if kind == "R" else ()
            copies.append((flow, (kind, side, d, *core, s), (kind, side ^ flip, wrap(d + shift), *core, s)))
    return copies


def most_left(rows, cols):
    counts = []
    for n in range(4 * RING * RING):
        x_lo, x_hi, y, z = n % 2, n // 2 % 2, n // 4 % RING, n // 4 // RING
        left = 0
        for k in range(BLOCKS):
            r = (k % 2 + x_hi) % 2 * RING + (k // 2 - z) % RING
            c = (k // RING + x_lo) % 2 * RING + (k % RING - y) % RING
            left += 1 - ((rows >> r) % 2) * ((cols >> c) % 2)
        counts.append(left)
    return max(counts)


def kernel(edge_hbm, tile_hbm, out_ref, edge_ref, tile_ref, turn_ref, rows_ref, cols_ref, total_ref, load_sem, send_sem, recv_sem):
    row, z, layer = lax.axis_index("row"), lax.axis_index("col"), lax.axis_index("layer")
    x_lo, y = row // RING, row % RING
    x_hi, core = layer // 2, layer % 2
    height, breadth = edge_ref.shape

    def turn(a, d):
        return (a + (d + RING)) % RING

    devices = {
        "yp": (x_lo * RING + turn(y, 1), z, layer),
        "ym": (x_lo * RING + turn(y, -1), z, layer),
        "zp": (row, turn(z, 1), layer),
        "zm": (row, turn(z, -1), layer),
        "lo": ((1 - x_lo) * RING + y, z, layer),
        "hi": (row, z, (1 - x_hi) * 2 + core),
        "sib": (row, z, x_hi * 2 + 1 - core),
    }
    barrier = pltpu.get_barrier_semaphore()
    for device in devices.values():
        pl.semaphore_signal(barrier, inc=1, device_id=device, device_id_type=MESH)

    loads = [
        pltpu.make_async_copy(tile_hbm, tile_ref, load_sem.at[0]),
        pltpu.make_async_copy(edge_hbm, edge_ref, load_sem.at[1]),
    ]
    for load in loads:
        load.start()
    for load in loads:
        load.wait()
    tile_cols, tile_rows = tile_ref.shape
    tile = height // tile_rows
    mine = z * 4 + layer
    for i in range(tile_rows):
        for j in range(tile_cols):
            stored = tile_ref[j, i] == 1
            at = (pl.ds(i * tile, tile), pl.ds(j * tile, tile))
            block = edge_ref[at]
            block = jnp.where(stored, block, jnp.zeros_like(block))
            rows_ref[(mine, *at)] = block
            cols_ref[(row, *at)] = block
    pl.semaphore_wait(barrier, len(devices))

    def place(piece):
        first, parts = piece[-1] if isinstance(piece[-1], tuple) else (piece[-1], 1)
        span = pl.ds(CUTS[first], CUTS[first + parts] - CUTS[first])
        if piece[0] == "C":
            _, side, d, _ = piece
            index = (x_lo if side == 0 else 1 - x_lo) * RING + turn(y, d)
            return cols_ref.at[index, span]
        _, side, d, k, _ = piece
        index = turn(z, d) * 4 + (x_hi if side == 0 else 1 - x_hi) * 2 + (core if k == 0 else 1 - core)
        return rows_ref.at[index, span]

    copies = copies_of(STEPS)
    arrivals = {copy[2]: n for n, copy in enumerate(copies)}
    waited = set()

    def arrive(piece):
        if piece not in arrivals or piece in waited:
            return
        waited.add(piece)
        n = arrivals[piece]
        there = place(piece)
        pltpu.make_async_remote_copy(
            src_ref=there, dst_ref=there, send_sem=send_sem.at[n], recv_sem=recv_sem.at[n],
            device_id=devices[copies[n][0]], device_id_type=MESH,
        ).wait_recv()

    def rank(k, carry):
        r = (k % 2 + x_hi) % 2 * RING + (k // 2 - z + RING) % RING
        c = (k // RING + x_lo) % 2 * RING + (k % RING - y + RING) % RING
        late = 0
        for rows, cols in turns[:-1]:
            late = late + 1 - ((rows >> r) % 2) * ((cols >> c) % 2)
        turn_ref[k] = late
        return carry

    def multiply(now):
        def step(k, carry):
            @pl.when(turn_ref[k] == now)
            def _():
                left = jnp.concatenate([rows_ref[2 * k], rows_ref[2 * k + 1]], axis=1)
                total_ref[...] += jnp.dot(left, cols_ref[k], preferred_element_type=jnp.float32)

            return carry

        lax.fori_loop(0, BLOCKS, step, 0)

    def picks(rows, cols):
        packed, base = 0 * row, 0 * row + 1
        for k in range(BLOCKS):
            r = (k % 2 + x_hi) % 2 * RING + (k // 2 - z + RING) % RING
            c = (k // RING + x_lo) % 2 * RING + (k % RING - y + RING) % RING
            hit = 1 - ((rows >> r) % 2) * ((cols >> c) % 2)
            packed = packed + hit * base * (k + 1)
            base = base * (1 + 31 * hit)
        return [(packed // 32**i % 32 + BLOCKS) % (BLOCKS + 1) for i in range(most_left(rows, cols))]

    def finish(slots):
        half = height // 2
        for m in range(2):
            span = pl.ds(m * half, half)
            total = total_ref[span, :]
            for slot in slots:
                k = slot % BLOCKS
                left = jnp.concatenate([rows_ref[2 * k, span, :], rows_ref[2 * k + 1, span, :]], axis=1)
                total += jnp.dot(left, cols_ref[slot], preferred_element_type=jnp.float32)
            out_ref[span, :] = total * cols_ref[row, span, :].astype(jnp.float32)

    order = {piece: n for n, piece in enumerate(copy[2] for copy in copies)}
    turns, started, now = [step[1:] for step in STEPS if step[0] == "mul"], [], 0
    for step in STEPS:
        if step[0] == "mul":
            _, rows, cols = step
            if now == len(turns) - 1:
                for copy in started[-LAG:-LAST]:
                    copy.wait_send()
                slots = picks(*turns[-2])
            ready = [p for p in order if ((rows if p[0] == "R" else cols) >> (RING * p[1] + p[2] % RING)) % 2]
            for piece in ready:
                arrive(piece)
            if now == 0:
                total_ref[...] = jnp.zeros_like(total_ref)
                cols_ref[BLOCKS] = jnp.zeros((height, breadth), cols_ref.dtype)
                lax.fori_loop(0, BLOCKS, rank, 0)
            if now == len(turns) - 1:
                finish(slots)
            else:
                multiply(now)
            now += 1
            continue
        n = len(started)
        flow, source, _ = copies[n]
        if flow == "sib":
            for s in range(source[-1][0], sum(source[-1])):
                arrive((*source[:-1], s))
        else:
            arrive(source)
        here = place(source)
        copy = pltpu.make_async_remote_copy(
            src_ref=here, dst_ref=here, send_sem=send_sem.at[n], recv_sem=recv_sem.at[n],
            device_id=devices[flow], device_id_type=MESH,
        )
        copy.start()
        started.append(copy)
        if n >= LAG:
            started[n - LAG].wait_send()
    for copy in started[-LAST:]:
        copy.wait_send()


def shards(edge_values, tile_pattern):
    height, breadth = edge_values.shape
    count = len(copies_of(STEPS))
    return pl.pallas_call(
        kernel,
        out_shape=jax.ShapeDtypeStruct((height, breadth), jnp.float32),
        in_specs=[pl.BlockSpec(memory_space=pl.ANY), pl.BlockSpec(memory_space=pl.ANY)],
        out_specs=pl.BlockSpec(memory_space=pltpu.VMEM),
        scratch_shapes=[
            pltpu.VMEM((height, breadth), edge_values.dtype),
            pltpu.SMEM(tile_pattern.shape[::-1], tile_pattern.dtype),
            pltpu.SMEM((BLOCKS,), jnp.int32),
            pltpu.VMEM((32, height, breadth), jnp.bfloat16),
            pltpu.VMEM((BLOCKS + 1, height, breadth), jnp.bfloat16),
            pltpu.VMEM((height, breadth), jnp.float32),
            pltpu.SemaphoreType.DMA((2,)),
            pltpu.SemaphoreType.DMA((count,)),
            pltpu.SemaphoreType.DMA((count,)),
        ],
        compiler_params=pltpu.CompilerParams(
            collective_id=0, has_side_effects=True, vmem_limit_bytes=24 * 1024 * 1024
        ),
        cost_estimate=pl.CostEstimate(flops=2 * height * 8192 * breadth, bytes_accessed=1 << 20, transcendentals=0),
    )(*(pltpu.with_memory_space_constraint(x, pltpu.HBM) for x in (edge_values, tile_pattern.T)))


def solution(mesh):
    return jax.shard_map(
        shards,
        mesh=mesh,
        in_specs=(P("row", ("col", "layer")), P("row", ("col", "layer"))),
        out_specs=P("row", ("col", "layer")),
        check_vma=False,
    )
```

```python
import jax
import jax.numpy as jnp
from jax import lax
from jax.experimental import pallas as pl
from jax.experimental.pallas import tpu as pltpu
from jax.sharding import PartitionSpec as P

MESH = pl.DeviceIdType.MESH
RING = 8
BLOCKS = 16
CUTS = (0, 128, 256, 384, 512)
LAG, LAST = 28, 8
FLOWS = {
    "ym": ("C", 0, 1), "yp": ("C", 0, -1), "lo": ("C", 1, 0),
    "zm": ("R", 0, 1), "zp": ("R", 0, -1), "hi": ("R", 1, 0),
}
STEPS = (
    ("ym", 0, 0, 0), ("yp", 0, 0, 0), ("zm", 0, 0, 0), ("zp", 0, 0, 0), ("lo", 0, 0, 0), ("ym", 0, 0, 1),
    ("yp", 0, 0, 1), ("zm", 0, 0, 1), ("zp", 0, 0, 1), ("lo", 0, 0, 1), ("ym", 0, 0, 2), ("yp", 0, 0, 2),
    ("zm", 0, 0, 2), ("zp", 0, 0, 2), ("lo", 0, 0, 2), ("ym", 0, 0, 3), ("yp", 0, 0, 3), ("zm", 0, 0, 3),
    ("zp", 0, 0, 3), ("lo", 0, 0, 3), ("sib", 0, 0, 0, 4), ("hi", 0, 0, 0), ("ym", 0, 1, 0), ("yp", 0, -1, 0),
    ("zm", 0, 1, 0), ("zp", 0, -1, 0), ("ym", 1, 0, 0), ("yp", 1, 0, 0), ("hi", 0, 1, 0), ("zm", 0, 1, 1),
    ("ym", 0, 1, 1), ("zp", 0, -1, 1), ("yp", 0, -1, 1), ("hi", 0, 1, 1), ("zm", 0, 1, 2), ("zp", 0, -1, 2),
    ("ym", 1, 0, 1), ("yp", 0, -1, 2), ("lo", 0, -1, 1), ("sib", 0, 1, 0, 4), ("zm", 0, 1, 3), ("sib", 0, -1, 0, 4),
    ("zp", 0, -1, 3), ("ym", 1, 0, 2), ("yp", 0, -1, 3), ("hi", 0, 1, 2), ("zm", 0, 2, 0), ("zp", 0, -2, 0),
    ("ym", 1, 0, 3), ("yp", 1, 0, 2), ("hi", 0, 1, 3), ("zp", 1, 0, 0), ("zm", 0, 2, 1), ("ym", 1, 1, 0),
    ("yp", 1, 0, 3), ("zp", 0, -2, 1), ("hi", 0, -2, 0), ("zm", 1, 1, 0), ("mul", 131, 387), ("ym", 0, 1, 2),
    ("yp", 0, -2, 0), ("zm", 0, 2, 2), ("zp", 0, -2, 2), ("hi", 0, -2, 1), ("sib", 0, 2, 0, 4), ("ym", 1, 1, 1),
    ("sib", 0, -2, 0, 4), ("yp", 0, -2, 1), ("zm", 0, 2, 3), ("zp", 1, 1, 1), ("hi", 0, -2, 2), ("ym", 1, 1, 2),
    ("yp", 0, -2, 2), ("zm", 1, 1, 1), ("zp", 0, -3, 0), ("hi", 0, 3, 0), ("mul", 131, 451), ("ym", 1, 1, 3),
    ("yp", 0, -2, 3), ("zm", 1, 1, 2), ("zp", 1, 1, 2), ("hi", 0, 3, 1), ("sib", 1, 1, 0, 4), ("ym", 0, 1, 3),
    ("yp", 1, -1, 0), ("zm", 1, 1, 3), ("zp", 1, 1, 3), ("hi", 0, -2, 3), ("ym", 1, 2, 0), ("yp", 0, -3, 0),
    ("zm", 0, 3, 1), ("zp", 1, -2, 0), ("hi", 0, 3, 2), ("mul", 199, 33731), ("sib", 0, 3, 0, 4),
    ("ym", 1, 2, 1), ("yp", 0, -3, 1), ("zm", 1, -2, 1), ("zp", 1, -2, 1), ("hi", 0, 3, 3), ("ym", 1, 2, 2),
    ("yp", 0, -3, 2), ("zm", 1, -2, 2), ("zp", 1, -2, 2), ("lo", 0, -3, 0), ("mul", 711, 33731), ("ym", 1, 2, 3),
    ("yp", 0, -3, 3), ("zm", 0, 3, 2), ("zp", 0, -2, 3), ("lo", 0, -3, 1), ("sib", 1, 2, 0, 4), ("ym", 0, 2, 0),
    ("sib", 1, 0, 0, 4), ("yp", 1, -1, 1), ("zm", 0, 3, 3), ("zp", 1, 0, 3), ("lo", 0, -3, 2), ("mul", 719, 34791),
    ("sib", 1, -2, 0, 4), ("ym", 1, 3, 0), ("sib", 1, -3, 0, 1), ("yp", 1, -1, 2), ("zm", 1, 3, 0),
    ("zp", 1, -2, 3), ("lo", 0, -3, 3), ("ym", 1, 3, 1), ("sib", 1, -3, 1, 1), ("yp", 0, 4, 1), ("zm", 1, 3, 1),
    ("lo", 0, -2, 3), ("sib", 1, 3, 0, 4), ("mul", 18383, 34791), ("ym", 1, 3, 2), ("sib", 1, -3, 2, 1),
    ("zp", 1, -3, 2), ("yp", 0, 4, 2), ("zm", 1, 3, 3), ("lo", 0, 4, 3), ("ym", 0, 2, 3), ("sib", 0, -3, 0, 4),
    ("mul", 18383, 34791), ("sib", 0, 4, 0, 4), ("sib", 1, -1, 0, 4), ("mul", 20431, 36855), ("sib", 1, 4, 0, 1),
    ("sib", 1, -3, 3, 1), ("sib", 1, 4, 1, 1), ("sib", 1, 4, 2, 1), ("sib", 1, 4, 3, 1), ("mul", 20479, 45047),
    ("mul", 61439, 61431), ("mul", 65535, 65535),
)


def wrap(d):
    return (d + RING // 2 - 1) % RING - (RING // 2 - 1)


def copies_of(steps):
    copies = []
    for flow, *rest in steps:
        if flow == "sib":
            side, d, s, n = rest
            copies.append((flow, ("R", side, d, 0, (s, n)), ("R", side, d, 1, (s, n))))
        elif flow != "mul":
            side, d, s = rest
            kind, flip, shift = FLOWS[flow]
            core = (0,) if kind == "R" else ()
            copies.append((flow, (kind, side, d, *core, s), (kind, side ^ flip, wrap(d + shift), *core, s)))
    return copies


def most_left(rows, cols):
    counts = []
    for n in range(4 * RING * RING):
        x_lo, x_hi, y, z = n % 2, n // 2 % 2, n // 4 % RING, n // 4 // RING
        left = 0
        for k in range(BLOCKS):
            r = (k % 2 + x_hi) % 2 * RING + (k // 2 - z) % RING
            c = (k // RING + x_lo) % 2 * RING + (k % RING - y) % RING
            left += 1 - ((rows >> r) % 2) * ((cols >> c) % 2)
        counts.append(left)
    return max(counts)


def kernel(edge_hbm, tile_hbm, out_ref, edge_ref, tile_ref, turn_ref, rows_ref, cols_ref, total_ref, load_sem, send_sem, recv_sem):
    row, z, layer = lax.axis_index("row"), lax.axis_index("col"), lax.axis_index("layer")
    x_lo, y = row // RING, row % RING
    x_hi, core = layer // 2, layer % 2
    height, breadth = edge_ref.shape

    def turn(a, d):
        return (a + (d + RING)) % RING

    devices = {
        "yp": (x_lo * RING + turn(y, 1), z, layer),
        "ym": (x_lo * RING + turn(y, -1), z, layer),
        "zp": (row, turn(z, 1), layer),
        "zm": (row, turn(z, -1), layer),
        "lo": ((1 - x_lo) * RING + y, z, layer),
        "hi": (row, z, (1 - x_hi) * 2 + core),
        "sib": (row, z, x_hi * 2 + 1 - core),
    }
    barrier = pltpu.get_barrier_semaphore()
    for device in devices.values():
        pl.semaphore_signal(barrier, inc=1, device_id=device, device_id_type=MESH)

    loads = [
        pltpu.make_async_copy(tile_hbm, tile_ref, load_sem.at[0]),
        pltpu.make_async_copy(edge_hbm, edge_ref, load_sem.at[1]),
    ]
    for load in loads:
        load.start()
    for load in loads:
        load.wait()
    tile_cols, tile_rows = tile_ref.shape
    tile = height // tile_rows
    mine = z * 4 + layer
    for i in range(tile_rows):
        for j in range(tile_cols):
            stored = tile_ref[j, i] == 1
            at = (pl.ds(i * tile, tile), pl.ds(j * tile, tile))
            block = edge_ref[at]
            block = jnp.where(stored, block, jnp.zeros_like(block))
            rows_ref[(mine, *at)] = block
            cols_ref[(row, *at)] = block
    pl.semaphore_wait(barrier, len(devices))

    def place(piece):
        first, parts = piece[-1] if isinstance(piece[-1], tuple) else (piece[-1], 1)
        span = pl.ds(CUTS[first], CUTS[first + parts] - CUTS[first])
        if piece[0] == "C":
            _, side, d, _ = piece
            index = (x_lo if side == 0 else 1 - x_lo) * RING + turn(y, d)
            return cols_ref.at[index, span]
        _, side, d, k, _ = piece
        index = turn(z, d) * 4 + (x_hi if side == 0 else 1 - x_hi) * 2 + (core if k == 0 else 1 - core)
        return rows_ref.at[index, span]

    copies = copies_of(STEPS)
    arrivals = {copy[2]: n for n, copy in enumerate(copies)}
    waited = set()

    def arrive(piece):
        if piece not in arrivals or piece in waited:
            return
        waited.add(piece)
        n = arrivals[piece]
        there = place(piece)
        pltpu.make_async_remote_copy(
            src_ref=there, dst_ref=there, send_sem=send_sem.at[n], recv_sem=recv_sem.at[n],
            device_id=devices[copies[n][0]], device_id_type=MESH,
        ).wait_recv()

    def rank(k, carry):
        r = (k % 2 + x_hi) % 2 * RING + (k // 2 - z + RING) % RING
        c = (k // RING + x_lo) % 2 * RING + (k % RING - y + RING) % RING
        late = 0
        for rows, cols in turns[:-1]:
            late = late + 1 - ((rows >> r) % 2) * ((cols >> c) % 2)
        turn_ref[k] = late
        return carry

    def multiply(now):
        def step(k, carry):
            @pl.when(turn_ref[k] == now)
            def _():
                left = jnp.concatenate([rows_ref[2 * k], rows_ref[2 * k + 1]], axis=1)
                total_ref[...] += jnp.dot(left, cols_ref[k], preferred_element_type=jnp.float32)

            return carry

        lax.fori_loop(0, BLOCKS, step, 0)

    def picks(rows, cols):
        packed, base = 0 * row, 0 * row + 1
        for k in range(BLOCKS):
            r = (k % 2 + x_hi) % 2 * RING + (k // 2 - z + RING) % RING
            c = (k // RING + x_lo) % 2 * RING + (k % RING - y + RING) % RING
            hit = 1 - ((rows >> r) % 2) * ((cols >> c) % 2)
            packed = packed + hit * base * (k + 1)
            base = base * (1 + 31 * hit)
        return [(packed // 32**i % 32 + BLOCKS) % (BLOCKS + 1) for i in range(most_left(rows, cols))]

    def finish(slots):
        half = height // 2
        for m in range(2):
            span = pl.ds(m * half, half)
            total = total_ref[span, :]
            for slot in slots:
                k = slot % BLOCKS
                left = jnp.concatenate([rows_ref[2 * k, span, :], rows_ref[2 * k + 1, span, :]], axis=1)
                total += jnp.dot(left, cols_ref[slot], preferred_element_type=jnp.float32)
            out_ref[span, :] = total * cols_ref[row, span, :].astype(jnp.float32)

    order = {piece: n for n, piece in enumerate(copy[2] for copy in copies)}
    turns, started, now = [step[1:] for step in STEPS if step[0] == "mul"], [], 0
    for step in STEPS:
        if step[0] == "mul":
            _, rows, cols = step
            if now == len(turns) - 1:
                for copy in started[-LAG:-LAST]:
                    copy.wait_send()
                slots = picks(*turns[-2])
            ready = [p for p in order if ((rows if p[0] == "R" else cols) >> (RING * p[1] + p[2] % RING)) % 2]
            for piece in ready:
                arrive(piece)
            if now == 0:
                total_ref[...] = jnp.zeros_like(total_ref)
                cols_ref[BLOCKS] = jnp.zeros((height, breadth), cols_ref.dtype)
                lax.fori_loop(0, BLOCKS, rank, 0)
            if now == len(turns) - 1:
                finish(slots)
            else:
                multiply(now)
            now += 1
            continue
        n = len(started)
        flow, source, _ = copies[n]
        if flow == "sib":
            for s in range(source[-1][0], sum(source[-1])):
                arrive((*source[:-1], s))
        else:
            arrive(source)
        here = place(source)
        copy = pltpu.make_async_remote_copy(
            src_ref=here, dst_ref=here, send_sem=send_sem.at[n], recv_sem=recv_sem.at[n],
            device_id=devices[flow], device_id_type=MESH,
        )
        copy.start()
        started.append(copy)
        if n >= LAG:
            started[n - LAG].wait_send()
    for copy in started[-LAST:]:
        copy.wait_send()


def shards(edge_values, tile_pattern):
    height, breadth = edge_values.shape
    count = len(copies_of(STEPS))
    return pl.pallas_call(
        kernel,
        out_shape=jax.ShapeDtypeStruct((height, breadth), jnp.float32),
        in_specs=[pl.BlockSpec(memory_space=pl.ANY), pl.BlockSpec(memory_space=pl.ANY)],
        out_specs=pl.BlockSpec(memory_space=pltpu.VMEM),
        scratch_shapes=[
            pltpu.VMEM((height, breadth), edge_values.dtype),
            pltpu.SMEM(tile_pattern.shape[::-1], tile_pattern.dtype),
            pltpu.SMEM((BLOCKS,), jnp.int32),
            pltpu.VMEM((32, height, breadth), jnp.bfloat16),
            pltpu.VMEM((BLOCKS + 1, height, breadth), jnp.bfloat16),
            pltpu.VMEM((height, breadth), jnp.float32),
            pltpu.SemaphoreType.DMA((2,)),
            pltpu.SemaphoreType.DMA((count,)),
            pltpu.SemaphoreType.DMA((count,)),
        ],
        compiler_params=pltpu.CompilerParams(
            collective_id=0, has_side_effects=True, vmem_limit_bytes=24 * 1024 * 1024
        ),
        cost_estimate=pl.CostEstimate(flops=2 * height * 8192 * breadth, bytes_accessed=1 << 20, transcendentals=0),
    )(*(pltpu.with_memory_space_constraint(x, pltpu.HBM) for x in (edge_values, tile_pattern.T)))


def solution(mesh):
    return jax.shard_map(
        shards,
        mesh=mesh,
        in_specs=(P("row", ("col", "layer")), P("row", ("col", "layer"))),
        out_specs=P("row", ("col", "layer")),
        check_vma=False,
    )
```

```python
import jax
import jax.numpy as jnp
from jax import lax
from jax.experimental import pallas as pl
from jax.experimental.pallas import tpu as pltpu
from jax.sharding import PartitionSpec as P

MESH = pl.DeviceIdType.MESH
RING = 8
BLOCKS = 16
CUTS = (0, 128, 256, 384, 512)
LAG, LAST = 28, 8
FLOWS = {
    "ym": ("C", 0, 1), "yp": ("C", 0, -1), "lo": ("C", 1, 0),
    "zm": ("R", 0, 1), "zp": ("R", 0, -1), "hi": ("R", 1, 0),
}
STEPS = (
    ("ym", 0, 0, 0), ("yp", 0, 0, 0), ("zm", 0, 0, 0), ("zp", 0, 0, 0), ("lo", 0, 0, 0), ("ym", 0, 0, 1),
    ("yp", 0, 0, 1), ("zm", 0, 0, 1), ("zp", 0, 0, 1), ("lo", 0, 0, 1), ("ym", 0, 0, 2), ("yp", 0, 0, 2),
    ("zm", 0, 0, 2), ("zp", 0, 0, 2), ("lo", 0, 0, 2), ("ym", 0, 0, 3), ("yp", 0, 0, 3), ("zm", 0, 0, 3),
    ("zp", 0, 0, 3), ("lo", 0, 0, 3), ("sib", 0, 0, 0, 4), ("hi", 0, 0, 0), ("ym", 0, 1, 0), ("yp", 0, -1, 0),
    ("zm", 0, 1, 0), ("zp", 0, -1, 0), ("ym", 1, 0, 0), ("yp", 1, 0, 0), ("hi", 0, 1, 0), ("zm", 0, 1, 1),
    ("ym", 0, 1, 1), ("zp", 0, -1, 1), ("yp", 0, -1, 1), ("hi", 0, 1, 1), ("zm", 0, 1, 2), ("zp", 0, -1, 2),
    ("ym", 1, 0, 1), ("yp", 0, -1, 2), ("lo", 0, -1, 1), ("sib", 0, 1, 0, 4), ("zm", 0, 1, 3), ("sib", 0, -1, 0, 4),
    ("zp", 0, -1, 3), ("ym", 1, 0, 2), ("yp", 0, -1, 3), ("hi", 0, 1, 2), ("zm", 0, 2, 0), ("zp", 0, -2, 0),
    ("ym", 1, 0, 3), ("yp", 1, 0, 2), ("hi", 0, 1, 3), ("zp", 1, 0, 0), ("zm", 0, 2, 1), ("ym", 1, 1, 0),
    ("yp", 1, 0, 3), ("zp", 0, -2, 1), ("hi", 0, -2, 0), ("zm", 1, 1, 0), ("mul", 131, 387), ("ym", 0, 1, 2),
    ("yp", 0, -2, 0), ("zm", 0, 2, 2), ("zp", 0, -2, 2), ("hi", 0, -2, 1), ("sib", 0, 2, 0, 4), ("ym", 1, 1, 1),
    ("sib", 0, -2, 0, 4), ("yp", 0, -2, 1), ("zm", 0, 2, 3), ("zp", 1, 1, 1), ("hi", 0, -2, 2), ("ym", 1, 1, 2),
    ("yp", 0, -2, 2), ("zm", 1, 1, 1), ("zp", 0, -3, 0), ("hi", 0, 3, 0), ("mul", 131, 451), ("ym", 1, 1, 3),
    ("yp", 0, -2, 3), ("zm", 1, 1, 2), ("zp", 1, 1, 2), ("hi", 0, 3, 1), ("sib", 1, 1, 0, 4), ("ym", 0, 1, 3),
    ("yp", 1, -1, 0), ("zm", 1, 1, 3), ("zp", 1, 1, 3), ("hi", 0, -2, 3), ("ym", 1, 2, 0), ("yp", 0, -3, 0),
    ("zm", 0, 3, 1), ("zp", 1, -2, 0), ("hi", 0, 3, 2), ("mul", 199, 33731), ("sib", 0, 3, 0, 4),
    ("ym", 1, 2, 1), ("yp", 0, -3, 1), ("zm", 1, -2, 1), ("zp", 1, -2, 1), ("hi", 0, 3, 3), ("ym", 1, 2, 2),
    ("yp", 0, -3, 2), ("zm", 1, -2, 2), ("zp", 1, -2, 2), ("lo", 0, -3, 0), ("mul", 711, 33731), ("ym", 1, 2, 3),
    ("yp", 0, -3, 3), ("zm", 0, 3, 2), ("zp", 0, -2, 3), ("lo", 0, -3, 1), ("sib", 1, 2, 0, 4), ("ym", 0, 2, 0),
    ("sib", 1, 0, 0, 4), ("yp", 1, -1, 1), ("zm", 0, 3, 3), ("zp", 1, 0, 3), ("lo", 0, -3, 2), ("mul", 719, 34791),
    ("sib", 1, -2, 0, 4), ("ym", 1, 3, 0), ("sib", 1, -3, 0, 1), ("yp", 1, -1, 2), ("zm", 1, 3, 0),
    ("zp", 1, -2, 3), ("lo", 0, -3, 3), ("ym", 1, 3, 1), ("sib", 1, -3, 1, 1), ("yp", 0, 4, 1), ("zm", 1, 3, 1),
    ("lo", 0, -2, 3), ("sib", 1, 3, 0, 4), ("mul", 18383, 34791), ("ym", 1, 3, 2), ("sib", 1, -3, 2, 1),
    ("zp", 1, -3, 2), ("yp", 0, 4, 2), ("zm", 1, 3, 3), ("lo", 0, 4, 3), ("ym", 0, 2, 3), ("sib", 0, -3, 0, 4),
    ("mul", 18383, 34791), ("sib", 0, 4, 0, 4), ("sib", 1, -1, 0, 4), ("sib", 1, 4, 0, 1), ("sib", 1, -3, 3, 1),
    ("mul", 20431, 36855), ("sib", 1, 4, 1, 1), ("sib", 1, 4, 2, 1), ("sib", 1, 4, 3, 1), ("mul", 20479, 45047),
    ("mul", 61439, 61431), ("mul", 65535, 65535),
)


def wrap(d):
    return (d + RING // 2 - 1) % RING - (RING // 2 - 1)


def copies_of(steps):
    copies = []
    for flow, *rest in steps:
        if flow == "sib":
            side, d, s, n = rest
            copies.append((flow, ("R", side, d, 0, (s, n)), ("R", side, d, 1, (s, n))))
        elif flow != "mul":
            side, d, s = rest
            kind, flip, shift = FLOWS[flow]
            core = (0,) if kind == "R" else ()
            copies.append((flow, (kind, side, d, *core, s), (kind, side ^ flip, wrap(d + shift), *core, s)))
    return copies


def most_left(rows, cols):
    counts = []
    for n in range(4 * RING * RING):
        x_lo, x_hi, y, z = n % 2, n // 2 % 2, n // 4 % RING, n // 4 // RING
        left = 0
        for k in range(BLOCKS):
            r = (k % 2 + x_hi) % 2 * RING + (k // 2 - z) % RING
            c = (k // RING + x_lo) % 2 * RING + (k % RING - y) % RING
            left += 1 - ((rows >> r) % 2) * ((cols >> c) % 2)
        counts.append(left)
    return max(counts)


def kernel(edge_hbm, tile_hbm, out_ref, edge_ref, tile_ref, turn_ref, rows_ref, cols_ref, total_ref, load_sem, send_sem, recv_sem):
    row, z, layer = lax.axis_index("row"), lax.axis_index("col"), lax.axis_index("layer")
    x_lo, y = row // RING, row % RING
    x_hi, core = layer // 2, layer % 2
    height, breadth = edge_ref.shape

    def turn(a, d):
        return (a + (d + RING)) % RING

    devices = {
        "yp": (x_lo * RING + turn(y, 1), z, layer),
        "ym": (x_lo * RING + turn(y, -1), z, layer),
        "zp": (row, turn(z, 1), layer),
        "zm": (row, turn(z, -1), layer),
        "lo": ((1 - x_lo) * RING + y, z, layer),
        "hi": (row, z, (1 - x_hi) * 2 + core),
        "sib": (row, z, x_hi * 2 + 1 - core),
    }
    barrier = pltpu.get_barrier_semaphore()
    for device in devices.values():
        pl.semaphore_signal(barrier, inc=1, device_id=device, device_id_type=MESH)

    loads = [
        pltpu.make_async_copy(tile_hbm, tile_ref, load_sem.at[0]),
        pltpu.make_async_copy(edge_hbm, edge_ref, load_sem.at[1]),
    ]
    for load in loads:
        load.start()
    for load in loads:
        load.wait()
    tile_cols, tile_rows = tile_ref.shape
    tile = height // tile_rows
    mine = z * 4 + layer
    for i in range(tile_rows):
        for j in range(tile_cols):
            stored = tile_ref[j, i] == 1
            at = (pl.ds(i * tile, tile), pl.ds(j * tile, tile))
            block = edge_ref[at]
            block = jnp.where(stored, block, jnp.zeros_like(block))
            rows_ref[(mine, *at)] = block
            cols_ref[(row, *at)] = block
    pl.semaphore_wait(barrier, len(devices))

    def place(piece):
        first, parts = piece[-1] if isinstance(piece[-1], tuple) else (piece[-1], 1)
        span = pl.ds(CUTS[first], CUTS[first + parts] - CUTS[first])
        if piece[0] == "C":
            _, side, d, _ = piece
            index = (x_lo if side == 0 else 1 - x_lo) * RING + turn(y, d)
            return cols_ref.at[index, span]
        _, side, d, k, _ = piece
        index = turn(z, d) * 4 + (x_hi if side == 0 else 1 - x_hi) * 2 + (core if k == 0 else 1 - core)
        return rows_ref.at[index, span]

    copies = copies_of(STEPS)
    arrivals = {copy[2]: n for n, copy in enumerate(copies)}
    waited = set()

    def arrive(piece):
        if piece not in arrivals or piece in waited:
            return
        waited.add(piece)
        n = arrivals[piece]
        there = place(piece)
        pltpu.make_async_remote_copy(
            src_ref=there, dst_ref=there, send_sem=send_sem.at[n], recv_sem=recv_sem.at[n],
            device_id=devices[copies[n][0]], device_id_type=MESH,
        ).wait_recv()

    def rank(k, carry):
        r = (k % 2 + x_hi) % 2 * RING + (k // 2 - z + RING) % RING
        c = (k // RING + x_lo) % 2 * RING + (k % RING - y + RING) % RING
        late = 0
        for rows, cols in turns[:-1]:
            late = late + 1 - ((rows >> r) % 2) * ((cols >> c) % 2)
        turn_ref[k] = late
        return carry

    def multiply(now):
        def step(k, carry):
            @pl.when(turn_ref[k] == now)
            def _():
                left = jnp.concatenate([rows_ref[2 * k], rows_ref[2 * k + 1]], axis=1)
                total_ref[...] += jnp.dot(left, cols_ref[k], preferred_element_type=jnp.float32)

            return carry

        lax.fori_loop(0, BLOCKS, step, 0)

    def picks(rows, cols):
        packed, base = 0 * row, 0 * row + 1
        for k in range(BLOCKS):
            r = (k % 2 + x_hi) % 2 * RING + (k // 2 - z + RING) % RING
            c = (k // RING + x_lo) % 2 * RING + (k % RING - y + RING) % RING
            hit = 1 - ((rows >> r) % 2) * ((cols >> c) % 2)
            packed = packed + hit * base * (k + 1)
            base = base * (1 + 31 * hit)
        return [(packed // 32**i % 32 + BLOCKS) % (BLOCKS + 1) for i in range(most_left(rows, cols))]

    def finish(slots):
        half = height // 2
        for m in range(2):
            span = pl.ds(m * half, half)
            total = total_ref[span, :]
            for slot in slots:
                k = slot % BLOCKS
                left = jnp.concatenate([rows_ref[2 * k, span, :], rows_ref[2 * k + 1, span, :]], axis=1)
                total += jnp.dot(left, cols_ref[slot], preferred_element_type=jnp.float32)
            out_ref[span, :] = total * cols_ref[row, span, :].astype(jnp.float32)

    order = {piece: n for n, piece in enumerate(copy[2] for copy in copies)}
    turns, started, now = [step[1:] for step in STEPS if step[0] == "mul"], [], 0
    for step in STEPS:
        if step[0] == "mul":
            _, rows, cols = step
            if now == len(turns) - 1:
                for copy in started[-LAG:-LAST]:
                    copy.wait_send()
                slots = picks(*turns[-2])
            ready = [p for p in order if ((rows if p[0] == "R" else cols) >> (RING * p[1] + p[2] % RING)) % 2]
            for piece in ready:
                arrive(piece)
            if now == 0:
                total_ref[...] = jnp.zeros_like(total_ref)
                cols_ref[BLOCKS] = jnp.zeros((height, breadth), cols_ref.dtype)
                lax.fori_loop(0, BLOCKS, rank, 0)
            if now == len(turns) - 1:
                finish(slots)
            else:
                multiply(now)
            now += 1
            continue
        n = len(started)
        flow, source, _ = copies[n]
        if flow == "sib":
            for s in range(source[-1][0], sum(source[-1])):
                arrive((*source[:-1], s))
        else:
            arrive(source)
        here = place(source)
        copy = pltpu.make_async_remote_copy(
            src_ref=here, dst_ref=here, send_sem=send_sem.at[n], recv_sem=recv_sem.at[n],
            device_id=devices[flow], device_id_type=MESH,
        )
        copy.start()
        started.append(copy)
        if n >= LAG:
            started[n - LAG].wait_send()
    for copy in started[-LAST:]:
        copy.wait_send()


def shards(edge_values, tile_pattern):
    height, breadth = edge_values.shape
    count = len(copies_of(STEPS))
    return pl.pallas_call(
        kernel,
        out_shape=jax.ShapeDtypeStruct((height, breadth), jnp.float32),
        in_specs=[pl.BlockSpec(memory_space=pl.ANY), pl.BlockSpec(memory_space=pl.ANY)],
        out_specs=pl.BlockSpec(memory_space=pltpu.VMEM),
        scratch_shapes=[
            pltpu.VMEM((height, breadth), edge_values.dtype),
            pltpu.SMEM(tile_pattern.shape[::-1], tile_pattern.dtype),
            pltpu.SMEM((BLOCKS,), jnp.int32),
            pltpu.VMEM((32, height, breadth), jnp.bfloat16),
            pltpu.VMEM((BLOCKS + 1, height, breadth), jnp.bfloat16),
            pltpu.VMEM((height, breadth), jnp.float32),
            pltpu.SemaphoreType.DMA((2,)),
            pltpu.SemaphoreType.DMA((count,)),
            pltpu.SemaphoreType.DMA((count,)),
        ],
        compiler_params=pltpu.CompilerParams(
            collective_id=0, has_side_effects=True, vmem_limit_bytes=24 * 1024 * 1024
        ),
        cost_estimate=pl.CostEstimate(flops=2 * height * 8192 * breadth, bytes_accessed=1 << 20, transcendentals=0),
    )(*(pltpu.with_memory_space_constraint(x, pltpu.HBM) for x in (edge_values, tile_pattern.T)))


def solution(mesh):
    return jax.shard_map(
        shards,
        mesh=mesh,
        in_specs=(P("row", ("col", "layer")), P("row", ("col", "layer"))),
        out_specs=P("row", ("col", "layer")),
        check_vma=False,
    )
```
